256 devices in a mesh: grid: 64 (over x_lo, z, y), orb: 4 (over x_hi, core).
Axes of the slice: x: 4 (x_hi: 2, x_lo: 2; x = x_hi * 2 + x_lo), y: 4, z: 8, core: 2. Of those that a mesh axis runs over, the one named last changes fastest.
Arguments:
- orbitals: float32 [16, 512, 32, 128], P('orb', 'grid'), may hold values from -6 to 6
- potential: float32 [512, 32, 128], P('grid'), may hold values from -1 to 1
Outputs:
- filtered: float32 [16, 512, 32, 128], P('orb', 'grid')
- correlation: float32 [16, 16], P('orb')
- hamiltonian: float32 [16, 16], P('orb')
The draws below stay inside these ranges and needn't reach their ends.
All inputs are finite; a program needn't handle non-finite values.
Results may differ from the reference program's by a relative error of at most 0.00005.
Values sent between devices are 32-bit elements; how exact they have to be, the bound alone decides.
A program may use at most 64 MiB of HBM per device.

```python
import jax
import jax.numpy as jnp
from jax import lax

NY = 32
NZ = 128
ORBS = 16
NX = 512


def block_levels(key, extent, shards, smallest, largest):
    level, own = 1.0, jax.random.fold_in(key, 6)
    for position, shards_of in shards:
        steps = jnp.exp(jax.random.uniform(jax.random.fold_in(own, position), (shards_of,), jnp.float32, smallest / len(shards), largest / len(shards)))
        level = level * jnp.repeat(steps, extent[position] // shards_of).reshape([-1 if axis == position else 1 for axis in range(len(extent))])
    return level


def gaussian(own_key, extent, scale, reach, split=(), held_as=jnp.bfloat16):
    loudness = block_levels(own_key, extent, split, -0.22, 0.18) if split else 1.0
    drawn = jax.random.normal(own_key, extent, jnp.float32) * scale * loudness
    return jnp.minimum(jnp.maximum(drawn, -reach), reach).astype(held_as)


def setup_inputs(seed: int = 0) -> dict:
    key_of = jax.random.split(jax.random.key(seed), 3)
    orbitals = gaussian(key_of[0], (ORBS, NX, NY, NZ), 1.0, 6.0, ((0, 4), (1, 64)), jnp.float32)
    potential = jnp.clip(jax.random.uniform(key_of[1], (NX, NY, NZ), jnp.float32, -1.0, 1.0) * block_levels(key_of[1], (NX, NY, NZ), ((0, 64),), -0.4, 0.0), -1.0, 1.0)
    return {"orbitals": orbitals, "potential": potential}


COEFS = (-205.0 / 72.0, 8.0 / 5.0, -1.0 / 5.0, 8.0 / 315.0, -1.0 / 560.0)
LOWER = -1.0
CUT = 4.0
UPPER = 10.0


def apply_ham(field, potential):
    lap = 3.0 * COEFS[0] * field
    for axis_pos in range(3):
        for shift_by in range(1, 5):
            lap = lap + COEFS[shift_by] * (jnp.roll(field, shift_by, axis_pos) + jnp.roll(field, -shift_by, axis_pos))
    return -0.5 * lap + potential * field


def filter_one(start, potential):
    half = (UPPER - CUT) / 2.0
    centre = (UPPER + CUT) / 2.0
    first_sigma = half / (LOWER - centre)
    previous = start
    current = (apply_ham(start, potential) - centre * start) * (first_sigma / half)
    sigma = first_sigma
    for step in range(3):
        sigma_new = 1.0 / (2.0 / first_sigma - sigma)
        following = (2.0 * sigma_new / half) * (apply_ham(current, potential) - centre * current) - (sigma * sigma_new) * previous
        previous = current
        current = following
        sigma = sigma_new
    return current, apply_ham(current, potential)


def reference(orbitals, potential):
    filtered, applied = lax.map(lambda start: filter_one(start, potential), orbitals)
    count = orbitals.shape[0]
    cells = orbitals.shape[1] * orbitals.shape[2] * orbitals.shape[3]
    flat_y = filtered.reshape(count, cells)
    flat_h = applied.reshape(count, cells)
    correlation = jnp.dot(flat_y, flat_y.T, precision=lax.Precision.HIGHEST) / cells
    hamiltonian = jnp.dot(flat_h, flat_y.T, precision=lax.Precision.HIGHEST) / cells
    return filtered, correlation, hamiltonian
```

```python
import jax
import jax.numpy as jnp
from jax import lax
from jax.experimental import pallas as pl
from jax.experimental.pallas import tpu as pltpu
from jax.sharding import PartitionSpec as P

COEFS = (-205.0 / 72.0, 8.0 / 5.0, -1.0 / 5.0, 8.0 / 315.0, -1.0 / 560.0)
LOWER = -1.0
CUT = 4.0
UPPER = 10.0

HALF = (UPPER - CUT) / 2.0
CENTRE = (UPPER + CUT) / 2.0
SIGMA_1 = HALF / (LOWER - CENTRE)


def chebyshev_factors():
    factors = [(SIGMA_1 / HALF, 0.0)]
    sigma = SIGMA_1
    for _ in range(3):
        sigma_new = 1.0 / (2.0 / SIGMA_1 - sigma)
        factors.append((2.0 * sigma_new / HALF, sigma * sigma_new))
        sigma = sigma_new
    return factors


FACTORS = chebyshev_factors()
REACH = 4
OWN = 8
NY = 32
NZ = 128
MESH = pl.DeviceIdType.MESH


def stencil_layer(src, orb, at, v_ref, v_at, scale, shift):
    here = src[orb, at]
    total = (scale * v_ref[v_at] + scale * (-shift - 1.5 * COEFS[0])) * here
    for k in range(1, REACH + 1):
        ring = src[orb, at + k] + src[orb, at - k]
        ring += pltpu.roll(here, k, 0) + pltpu.roll(here, NY - k, 0)
        ring += pltpu.roll(here, k, 1) + pltpu.roll(here, NZ - k, 1)
        total += (-0.5 * scale * COEFS[k]) * ring
    return total


def kernel(orbitals, potential, filtered, corr, ham,
           p0, p1, p2, p3, p4, hy, v_ref, every, acc, rows_1, rows_2,
           in_sem, v_send, v_recv, a_send, a_recv, b_send, b_recv, c_send, c_recv,
           x_send, x_recv, out_sem, r1_send, r1_recv, r2_send, r2_recv):
    g = lax.axis_index("grid")
    o = lax.axis_index("orb")
    x_lo, z, y = g // 32, (g // 4) % 8, g % 4
    up = (lax.rem(g + 1, 64), o)
    down = (lax.rem(g + 63, 64), o)
    o_core = o + 1 - 2 * lax.rem(o, 2)
    o_far = lax.rem(o + 2, 4)
    core = (g, o_core)
    far = (g, o_far)

    def peer_1(d):
        return (lax.rem(x_lo + d // 4, 2) * 32 + z * 4 + lax.rem(y + d % 4, 4), o)

    def peer_2(d):
        return (x_lo * 32 + lax.rem(z + d, 8) * 4 + y, o)

    barrier = pltpu.get_barrier_semaphore()
    partners = [up, down, core, far] + [peer_1(d) for d in range(1, 8)] + [peer_2(d) for d in range(1, 8)]
    for partner in partners:
        pl.semaphore_signal(barrier, inc=1, device_id=partner, device_id_type=MESH)

    own_v = pltpu.make_async_copy(potential, v_ref.at[pl.ds(REACH, OWN)], in_sem.at[4])
    own_v.start()
    own_in = [pltpu.make_async_copy(orbitals.at[i], p0.at[i, pl.ds(OWN, OWN)], in_sem.at[i]) for i in range(4)]
    for copy in own_in:
        copy.start()

    pl.semaphore_wait(barrier, len(partners))

    def remote(src, dst, send, recv, device):
        return pltpu.make_async_remote_copy(
            src_ref=src, dst_ref=dst, send_sem=send, recv_sem=recv, device_id=device, device_id_type=MESH
        )

    v_copies = [
        remote(potential.at[pl.ds(OWN - REACH, REACH)], v_ref.at[pl.ds(0, REACH)], v_send.at[0], v_recv.at[0], up),
        remote(potential.at[pl.ds(0, REACH)], v_ref.at[pl.ds(REACH + OWN, REACH)], v_send.at[1], v_recv.at[1], down),
    ]
    a_copies = [
        [
            remote(orbitals.at[i], p0.at[i, pl.ds(0, OWN)], a_send.at[i, 0], a_recv.at[i, 0], up),
            remote(orbitals.at[i], p0.at[i, pl.ds(2 * OWN, OWN)], a_send.at[i, 1], a_recv.at[i, 1], down),
        ]
        for i in range(4)
    ]
    b_copies = [
        [
            remote(p2.at[i, pl.ds(OWN, OWN)], p2.at[i, pl.ds(0, OWN)], b_send.at[i, 0], b_recv.at[i, 0], up),
            remote(p2.at[i, pl.ds(OWN, OWN)], p2.at[i, pl.ds(2 * OWN, OWN)], b_send.at[i, 1], b_recv.at[i, 1], down),
        ]
        for i in range(4)
    ]
    c_copies = [
        [
            remote(p4.at[i, pl.ds(OWN, REACH)], p4.at[i, pl.ds(0, REACH)], c_send.at[i, 0], c_recv.at[i, 0], up),
            remote(p4.at[i, pl.ds(REACH, REACH)], p4.at[i, pl.ds(REACH + OWN, REACH)], c_send.at[i, 1], c_recv.at[i, 1], down),
        ]
        for i in range(4)
    ]
    x_copies = [
        [
            remote(every.at[o, i], every.at[o, i], x_send.at[i, 0], x_recv.at[i, 0], core),
            remote(every.at[o, i], every.at[o, i], x_send.at[i, 1], x_recv.at[i, 1], far),
            remote(every.at[o_far, i], every.at[o_far, i], x_send.at[i, 2], x_recv.at[i, 2], core),
        ]
        for i in range(4)
    ]
    out_copies = [pltpu.make_async_copy(every.at[o, i], filtered.at[i], out_sem.at[i]) for i in range(4)]

    def start(copies):
        for copy in copies:
            copy.start()

    def arrived(copies):
        for copy in copies:
            copy.wait_recv()

    def layers(count, body):
        def step(at, carry):
            body(at)
            return carry
        lax.fori_loop(0, count, step, 0, unroll=2)

    def unit_a(i):
        if i == 0:
            own_v.wait()
            arrived(v_copies)
        own_in[i].wait()
        arrived(a_copies[i])

        def first(at):
            p1[i, at] = stencil_layer(p0, i, at + REACH, v_ref, at, FACTORS[0][0], CENTRE)
        layers(2 * OWN, first)

        def second(at):
            p2[i, at + OWN] = stencil_layer(
                p1, i, at + REACH, v_ref, at + REACH, FACTORS[1][0], CENTRE
            ) - FACTORS[1][1] * p0[i, at + OWN]
        layers(OWN, second)
        start(b_copies[i])

    def unit_b(i):
        arrived(b_copies[i])

        def third(at):
            p3[i, at] = stencil_layer(
                p2, i, at + REACH, v_ref, at, FACTORS[2][0], CENTRE
            ) - FACTORS[2][1] * p1[i, at]
        layers(2 * OWN, third)

        def fourth(at):
            value = stencil_layer(
                p3, i, at + REACH, v_ref, at + REACH, FACTORS[3][0], CENTRE
            ) - FACTORS[3][1] * p2[i, at + OWN]
            p4[i, at + REACH] = value
            every[o, i, at] = value
        layers(OWN, fourth)
        start(c_copies[i])
        x_copies[i][1].start()
        x_copies[i][0].start()
        out_copies[i].start()

    def unit_c(i):
        arrived(c_copies[i])

        def applied(at):
            hy[i, at] = stencil_layer(p4, i, at + REACH, v_ref, at + REACH, 1.0, 0.0)
        layers(OWN, applied)
        x_copies[i][1].wait_recv()
        x_copies[i][2].start()

    def products(fields, partners_of):
        def step(at, sums):
            sums = list(sums)
            for part in range(NY // 8):
                rows = pl.ds(part * 8, 8)
                left = [hy[i, at, rows, :] if kind else every[o, i, at, rows, :] for kind, i in fields]
                for n, (slot, j) in enumerate(partners_of):
                    right = every[slot, j, at, rows, :]
                    for m in range(len(fields)):
                        sums[m * len(partners_of) + n] += left[m] * right
            return tuple(sums)

        zero = jnp.zeros((8, NZ), jnp.float32)
        sums = lax.fori_loop(0, OWN, step, (zero,) * (len(fields) * len(partners_of)))
        for m, (kind, i) in enumerate(fields):
            for n, (slot, j) in enumerate(partners_of):
                acc[(kind * 4 + i) * 16 + slot * 4 + j] = sums[m * len(partners_of) + n]

    def unit_d(i):
        x_copies[i][0].wait_recv()
        x_copies[i][2].wait_recv()
        products([(0, i), (1, i)], [(slot, j) for slot in range(4) for j in range(i + 1)])
        if i:
            products([(kind, m) for kind in range(2) for m in range(i)], [(slot, i) for slot in range(4)])

    start(v_copies)
    start(a_copies[0])
    start(a_copies[1])
    start(a_copies[2])
    unit_a(0)
    start(a_copies[3])
    unit_a(1)
    unit_a(2)
    unit_b(0)
    unit_a(3)
    unit_b(1)
    unit_c(0)
    unit_d(0)
    unit_b(2)
    unit_c(1)
    unit_d(1)
    unit_b(3)
    unit_c(2)
    unit_d(2)
    unit_c(3)
    unit_d(3)

    sums = jnp.sum(acc[...], axis=1)
    flat = lax.dot_general(
        jnp.full((8, NZ), 1.0 / (512 * NY * NZ), jnp.float32), sums, (((1,), (1,)), ((), ())),
        precision=lax.Precision.HIGHEST, preferred_element_type=jnp.float32,
    )
    row = lax.broadcasted_iota(jnp.int32, (8, NZ), 0)
    tile = flat
    for r in range(1, 8):
        tile = jnp.where(row == r, pltpu.roll(flat, NZ - 16 * r, 1), tile)

    me_1 = x_lo * 4 + y
    rows_1[me_1] = tile
    copies_1 = [remote(rows_1.at[me_1], rows_1.at[me_1], r1_send.at[d - 1], r1_recv.at[d - 1], peer_1(d)) for d in range(1, 8)]
    start(copies_1)
    arrived(copies_1)
    rows_2[z] = jnp.sum(rows_1[...], axis=0)
    copies_2 = [remote(rows_2.at[z], rows_2.at[z], r2_send.at[d - 1], r2_recv.at[d - 1], peer_2(d)) for d in range(1, 8)]
    start(copies_2)
    arrived(copies_2)
    tile = jnp.sum(rows_2[...], axis=0)
    corr[...] = tile[0:4, 0:16]
    ham[...] = tile[4:8, 0:16]

    for copies in [v_copies, copies_1, copies_2] + a_copies + b_copies + c_copies + x_copies:
        for copy in copies:
            copy.wait_send()
    for copy in out_copies:
        copy.wait()


def per_device(orbitals, potential):
    dma = pltpu.SemaphoreType.DMA
    field = lambda count: pltpu.VMEM((4, count, NY, NZ), jnp.float32)
    return pl.pallas_call(
        kernel,
        out_shape=(
            jax.ShapeDtypeStruct((4, OWN, NY, NZ), jnp.float32),
            jax.ShapeDtypeStruct((4, 16), jnp.float32),
            jax.ShapeDtypeStruct((4, 16), jnp.float32),
        ),
        in_specs=[pl.BlockSpec(memory_space=pl.ANY)] * 2,
        out_specs=(
            pl.BlockSpec(memory_space=pl.ANY),
            pl.BlockSpec(memory_space=pltpu.VMEM),
            pl.BlockSpec(memory_space=pltpu.VMEM),
        ),
        scratch_shapes=[
            field(3 * OWN), field(2 * OWN), field(3 * OWN), field(2 * OWN), field(2 * OWN), field(OWN),
            pltpu.VMEM((2 * OWN, NY, NZ), jnp.float32),
            pltpu.VMEM((4, 4, OWN, NY, NZ), jnp.float32),
            pltpu.VMEM((128, 8, NZ), jnp.float32),
            pltpu.VMEM((8, 8, NZ), jnp.float32),
            pltpu.VMEM((8, 8, NZ), jnp.float32),
            dma((5,)), dma((2,)), dma((2,)),
            dma((4, 2)), dma((4, 2)), dma((4, 2)), dma((4, 2)), dma((4, 2)), dma((4, 2)),
            dma((4, 3)), dma((4, 3)), dma((4,)),
            dma((7,)), dma((7,)), dma((7,)), dma((7,)),
        ],
        compiler_params=pltpu.CompilerParams(
            collective_id=0, has_side_effects=True, vmem_limit_bytes=40 * 1024 * 1024
        ),
    )(orbitals, potential)


def solution(mesh):
    return jax.shard_map(
        per_device,
        mesh=mesh,
        in_specs=(P("orb", "grid", None, None), P("grid", None, None)),
        out_specs=(P("orb", "grid", None, None), P("orb", None), P("orb", None)),
        check_vma=False,
    )
```

```python
import jax
import jax.numpy as jnp
from jax import lax
from jax.experimental import pallas as pl
from jax.experimental.pallas import tpu as pltpu
from jax.sharding import PartitionSpec as P

COEFS = (-205.0 / 72.0, 8.0 / 5.0, -1.0 / 5.0, 8.0 / 315.0, -1.0 / 560.0)
LOWER = -1.0
CUT = 4.0
UPPER = 10.0

HALF = (UPPER - CUT) / 2.0
CENTRE = (UPPER + CUT) / 2.0
SIGMA_1 = HALF / (LOWER - CENTRE)


def chebyshev_factors():
    factors = [(SIGMA_1 / HALF, 0.0)]
    sigma = SIGMA_1
    for _ in range(3):
        sigma_new = 1.0 / (2.0 / SIGMA_1 - sigma)
        factors.append((2.0 * sigma_new / HALF, sigma * sigma_new))
        sigma = sigma_new
    return factors


FACTORS = chebyshev_factors()
REACH = 4
OWN = 8
NY = 32
NZ = 128
MESH = pl.DeviceIdType.MESH


EVEN = (COEFS[2] + COEFS[4]) / 2.0
ODD = (COEFS[4] - COEFS[2]) / 2.0


def stencil_layer(src, orb, at, v_ref, v_at, scale, shift):
    here = src[orb, at]
    factor = -0.5 * scale
    near = src[orb, at + 1] + src[orb, at - 1]
    third = (factor * COEFS[3]) * here
    total = (scale * v_ref[v_at] + scale * (-shift - 1.5 * COEFS[0])) * here
    for axis, size in ((1, NZ), (0, NY)):
        after, before = pltpu.roll(here, 1, axis), pltpu.roll(here, size - 1, axis)
        both = after + before
        even = third + (factor * EVEN) * both
        odd = (factor * ODD) * (after - before)
        near += both
        total += pltpu.roll(even + odd, 3, axis) + pltpu.roll(even - odd, size - 3, axis)
    total += (factor * COEFS[1]) * near
    for k in range(2, REACH + 1):
        total += (factor * COEFS[k]) * (src[orb, at + k] + src[orb, at - k])
    return total


def kernel(orbitals, potential, filtered, corr, ham,
           p0, p1, p2, p3, p4, hy, v_ref, every, acc, rows,
           in_sem, v_send, v_recv, a_send, a_recv, b_send, b_recv, c_send, c_recv,
           x_send, x_recv, out_sem, r_send, r_recv):
    g = lax.axis_index("grid")
    o = lax.axis_index("orb")
    x_lo, z, y = g // 32, (g // 4) % 8, g % 4
    up = (lax.rem(g + 1, 64), o)
    down = (lax.rem(g + 63, 64), o)
    o_core = o + 1 - 2 * lax.rem(o, 2)
    o_far = lax.rem(o + 2, 4)
    core = (g, o_core)
    far = (g, o_far)
    corner_up = (z == 7) & (y == 3) & (lax.rem(o, 2) == 1)
    corner_down = (z == 0) & (y == 0) & (lax.rem(o, 2) == 1)
    corner = corner_up | corner_down
    across = (lax.rem(g + 32, 64), o)
    onward = (x_lo * 32 + jnp.where(corner_up, 0, 31), o)
    up_first = (jnp.where(corner_up, across[0], up[0]), o)
    down_first = (jnp.where(corner_down, across[0], down[0]), o)
    up_at, up_sem = jnp.where(corner_up, 3 * OWN, 0), jnp.where(corner_up, 2, 0)
    down_at, down_sem = jnp.where(corner_down, 3 * OWN, 2 * OWN), jnp.where(corner_down, 2, 1)
    onward_at, onward_sem = jnp.where(corner_up, 0, 2 * OWN), jnp.where(corner_up, 0, 1)

    offsets = [(dx, dz, dy) for dx in range(2) for dz in range(8) for dy in range(4) if dx or dz or dy]
    offsets.sort(key=lambda d: -(d[0] + min(d[1], 8 - d[1]) + min(d[2], 4 - d[2])))
    others = [(lax.rem(x_lo + dx, 2) * 32 + lax.rem(z + dz, 8) * 4 + lax.rem(y + dy, 4), o) for dx, dz, dy in offsets]

    barrier = pltpu.get_barrier_semaphore()
    partners = others + [core, far]
    for partner in partners:
        pl.semaphore_signal(barrier, inc=1, device_id=partner, device_id_type=MESH)

    own_v = pltpu.make_async_copy(potential, v_ref.at[pl.ds(REACH, OWN)], in_sem.at[4])
    own_v.start()
    own_in = [pltpu.make_async_copy(orbitals.at[i], p0.at[i, pl.ds(OWN, OWN)], in_sem.at[i]) for i in range(4)]
    for copy in own_in:
        copy.start()

    pl.semaphore_wait(barrier, len(partners))

    def remote(src, dst, send, recv, device):
        return pltpu.make_async_remote_copy(
            src_ref=src, dst_ref=dst, send_sem=send, recv_sem=recv, device_id=device, device_id_type=MESH
        )

    v_copies = [
        remote(potential.at[pl.ds(OWN - REACH, REACH)], v_ref.at[pl.ds(0, REACH)], v_send.at[0], v_recv.at[0], up),
        remote(potential.at[pl.ds(0, REACH)], v_ref.at[pl.ds(REACH + OWN, REACH)], v_send.at[1], v_recv.at[1], down),
    ]

    def block_copies(i, src, dst, send, recv):
        return [
            remote(src, dst.at[i, pl.ds(up_at, OWN)], send.at[i, 0], recv.at[i, up_sem], up_first),
            remote(src, dst.at[i, pl.ds(down_at, OWN)], send.at[i, 1], recv.at[i, down_sem], down_first),
        ]

    def block_arrivals(i, dst, send, recv):
        return [
            remote(dst.at[i, pl.ds(0, OWN)], dst.at[i, pl.ds(0, OWN)], send.at[i, 0], recv.at[i, 0], up),
            remote(dst.at[i, pl.ds(2 * OWN, OWN)], dst.at[i, pl.ds(2 * OWN, OWN)], send.at[i, 1], recv.at[i, 1], down),
        ]

    def corner_copy(i, dst, send, recv):
        return remote(
            dst.at[i, pl.ds(3 * OWN, OWN)], dst.at[i, pl.ds(onward_at, OWN)],
            send.at[i, 2], recv.at[i, onward_sem], onward,
        )

    def send_onward(i, dst, send, recv):
        @pl.when(corner)
        def _():
            remote(
                dst.at[i, pl.ds(3 * OWN, OWN)], dst.at[i, pl.ds(3 * OWN, OWN)], send.at[i, 2], recv.at[i, 2], across
            ).wait_recv()
            corner_copy(i, dst, send, recv).start()

    a_copies = [block_copies(i, orbitals.at[i], p0, a_send, a_recv) for i in range(4)]
    a_arrivals = [block_arrivals(i, p0, a_send, a_recv) for i in range(4)]
    b_copies = [block_copies(i, p2.at[i, pl.ds(OWN, OWN)], p2, b_send, b_recv) for i in range(4)]
    b_arrivals = [block_arrivals(i, p2, b_send, b_recv) for i in range(4)]
    c_copies = [
        [
            remote(p4.at[i, pl.ds(OWN, REACH)], p4.at[i, pl.ds(0, REACH)], c_send.at[i, 0], c_recv.at[i, 0], up),
            remote(p4.at[i, pl.ds(REACH, REACH)], p4.at[i, pl.ds(REACH + OWN, REACH)], c_send.at[i, 1], c_recv.at[i, 1], down),
        ]
        for i in range(4)
    ]
    x_copies = [
        [
            remote(every.at[o, i], every.at[o, i], x_send.at[i, 0], x_recv.at[i, 0], core),
            remote(every.at[o, i], every.at[o, i], x_send.at[i, 1], x_recv.at[i, 1], far),
            remote(every.at[o_far, i], every.at[o_far, i], x_send.at[i, 2], x_recv.at[i, 2], core),
        ]
        for i in range(4)
    ]
    out_copies = [pltpu.make_async_copy(every.at[o, i], filtered.at[i], out_sem.at[i]) for i in range(4)]

    def start(copies):
        for copy in copies:
            copy.start()

    def arrived(copies):
        for copy in copies:
            copy.wait_recv()

    gone = []

    def sent(copies):
        for copy in copies:
            copy.wait_send()
        gone.append(copies)

    def layers(count, body):
        def step(at, carry):
            body(at)
            return carry
        lax.fori_loop(0, count, step, 0, unroll=8)

    def unit_a(i):
        if i == 0:
            own_v.wait()
            arrived(v_copies)
        own_in[i].wait()
        arrived(a_arrivals[i])

        def first(at):
            p1[i, at] = stencil_layer(p0, i, at + REACH, v_ref, at, FACTORS[0][0], CENTRE)
        layers(2 * OWN, first)

        def second(at):
            p2[i, at + OWN] = stencil_layer(
                p1, i, at + REACH, v_ref, at + REACH, FACTORS[1][0], CENTRE
            ) - FACTORS[1][1] * p0[i, at + OWN]
        layers(OWN, second)

    def unit_b(i):
        arrived(b_arrivals[i])

        def third(at):
            p3[i, at] = stencil_layer(
                p2, i, at + REACH, v_ref, at, FACTORS[2][0], CENTRE
            ) - FACTORS[2][1] * p1[i, at]
        layers(2 * OWN, third)

        def fourth(at):
            value = stencil_layer(
                p3, i, at + REACH, v_ref, at + REACH, FACTORS[3][0], CENTRE
            ) - FACTORS[3][1] * p2[i, at + OWN]
            p4[i, at + REACH] = value
            every[o, i, at] = value
        layers(OWN, fourth)
        x_copies[i][1].start()
        x_copies[i][0].start()
        out_copies[i].start()

    def unit_c(i):
        arrived(c_copies[i])

        def applied(at):
            hy[i, at] = stencil_layer(p4, i, at + REACH, v_ref, at + REACH, 1.0, 0.0)
        layers(OWN, applied)
        x_copies[i][1].wait_recv()
        x_copies[i][2].start()

    def products(fields, partners_of):
        def step(at, sums):
            sums = list(sums)
            for part in range(NY // 8):
                rows = pl.ds(part * 8, 8)
                left = [hy[i, at, rows, :] if kind else every[o, i, at, rows, :] for kind, i in fields]
                for n, (slot, j) in enumerate(partners_of):
                    right = every[slot, j, at, rows, :]
                    for m in range(len(fields)):
                        sums[m * len(partners_of) + n] += left[m] * right
            return tuple(sums)

        zero = jnp.zeros((8, NZ), jnp.float32)
        sums = lax.fori_loop(0, OWN, step, (zero,) * (len(fields) * len(partners_of)))
        for m, (kind, i) in enumerate(fields):
            for n, (slot, j) in enumerate(partners_of):
                acc[(kind * 4 + i) * 16 + slot * 4 + j] = sums[m * len(partners_of) + n]

    def unit_d(i):
        x_copies[i][0].wait_recv()
        x_copies[i][2].wait_recv()
        products([(0, i), (1, i)], [(slot, j) for slot in range(4) for j in range(i + 1)])
        if i:
            products([(kind, m) for kind in range(2) for m in range(i)], [(slot, i) for slot in range(4)])

    start(a_copies[0])
    start(v_copies)
    start(a_copies[1])
    start(a_copies[2])
    start(a_copies[3])
    send_onward(0, p0, a_send, a_recv)
    send_onward(1, p0, a_send, a_recv)
    send_onward(2, p0, a_send, a_recv)
    send_onward(3, p0, a_send, a_recv)
    unit_a(0)
    start(b_copies[0])
    unit_a(1)
    start(b_copies[1])
    send_onward(0, p2, b_send, b_recv)
    unit_a(2)
    start(b_copies[2])
    send_onward(1, p2, b_send, b_recv)
    unit_a(3)
    start(b_copies[3])
    send_onward(2, p2, b_send, b_recv)
    unit_b(0)
    start(c_copies[0])
    send_onward(3, p2, b_send, b_recv)
    unit_b(1)
    start(c_copies[1])
    unit_b(2)
    start(c_copies[2])
    unit_b(3)
    start(c_copies[3])
    unit_c(0)
    unit_c(1)
    unit_c(2)
    unit_d(0)
    unit_d(1)
    unit_d(2)
    unit_c(3)
    unit_d(3)

    sums = jnp.sum(acc[...], axis=1)
    flat = lax.dot_general(
        jnp.full((8, NZ), 1.0 / (512 * NY * NZ), jnp.float32), sums, (((1,), (1,)), ((), ())),
        precision=lax.Precision.HIGHEST, preferred_element_type=jnp.float32,
    )
    rows[pl.ds(g, 1)] = flat[0:1]
    sum_copies = [
        remote(rows.at[pl.ds(g, 1)], rows.at[pl.ds(g, 1)], r_send.at[n], r_recv.at[n], peer)
        for n, peer in enumerate(others)
    ]
    start(sum_copies)
    arrived(sum_copies)
    total = jnp.sum(rows[...], axis=0, keepdims=True)
    for kind, ref in ((0, corr), (1, ham)):
        for i in range(4):
            first = (kind * 4 + i) * 16
            ref[pl.ds(i, 1), :] = total[:, first : first + 16]

    for copies in [v_copies, sum_copies] + a_copies + b_copies + c_copies + x_copies:
        if not any(copies is other for other in gone):
            sent(copies)
    for copy in out_copies:
        copy.wait()

    @pl.when(corner)
    def _():
        for i in range(4):
            corner_copy(i, p0, a_send, a_recv).wait_send()
            corner_copy(i, p2, b_send, b_recv).wait_send()


def per_device(orbitals, potential):
    dma = pltpu.SemaphoreType.DMA
    field = lambda count: pltpu.VMEM((4, count, NY, NZ), jnp.float32)
    return pl.pallas_call(
        kernel,
        out_shape=(
            jax.ShapeDtypeStruct((4, OWN, NY, NZ), jnp.float32),
            jax.ShapeDtypeStruct((4, 16), jnp.float32),
            jax.ShapeDtypeStruct((4, 16), jnp.float32),
        ),
        in_specs=[pl.BlockSpec(memory_space=pl.ANY)] * 2,
        out_specs=(
            pl.BlockSpec(memory_space=pl.ANY),
            pl.BlockSpec(memory_space=pltpu.VMEM),
            pl.BlockSpec(memory_space=pltpu.VMEM),
        ),
        scratch_shapes=[
            field(4 * OWN), field(2 * OWN), field(4 * OWN), field(2 * OWN), field(2 * OWN), field(OWN),
            pltpu.VMEM((2 * OWN, NY, NZ), jnp.float32),
            pltpu.VMEM((4, 4, OWN, NY, NZ), jnp.float32),
            pltpu.VMEM((128, 8, NZ), jnp.float32),
            pltpu.VMEM((64, NZ), jnp.float32),
            dma((5,)), dma((2,)), dma((2,)),
            dma((4, 3)), dma((4, 3)), dma((4, 3)), dma((4, 3)), dma((4, 2)), dma((4, 2)),
            dma((4, 3)), dma((4, 3)), dma((4,)),
            dma((63,)), dma((63,)),
        ],
        compiler_params=pltpu.CompilerParams(
            collective_id=0, has_side_effects=True, vmem_limit_bytes=63 * 1024 * 1024
        ),
    )(orbitals, potential)


def solution(mesh):
    return jax.shard_map(
        per_device,
        mesh=mesh,
        in_specs=(P("orb", "grid", None, None), P("grid", None, None)),
        out_specs=(P("orb", "grid", None, None), P("orb", None), P("orb", None)),
        check_vma=False,
    )
```

```python
import jax
import jax.numpy as jnp
from jax import lax
from jax.experimental import pallas as pl
from jax.experimental.pallas import tpu as pltpu
from jax.sharding import PartitionSpec as P

COEFS = (-205.0 / 72.0, 8.0 / 5.0, -1.0 / 5.0, 8.0 / 315.0, -1.0 / 560.0)
LOWER = -1.0
CUT = 4.0
UPPER = 10.0

HALF = (UPPER - CUT) / 2.0
CENTRE = (UPPER + CUT) / 2.0
SIGMA_1 = HALF / (LOWER - CENTRE)


def chebyshev_factors():
    factors = [(SIGMA_1 / HALF, 0.0)]
    sigma = SIGMA_1
    for _ in range(3):
        sigma_new = 1.0 / (2.0 / SIGMA_1 - sigma)
        factors.append((2.0 * sigma_new / HALF, sigma * sigma_new))
        sigma = sigma_new
    return factors


FACTORS = chebyshev_factors()
REACH = 4
OWN = 8
NY = 32
NZ = 128
MESH = pl.DeviceIdType.MESH


EVEN = (COEFS[2] + COEFS[4]) / 2.0
ODD = (COEFS[4] - COEFS[2]) / 2.0


def stencil_layer(src, orb, at, v_ref, v_at, scale, shift):
    here = src[orb, at]
    factor = -0.5 * scale
    near = src[orb, at + 1] + src[orb, at - 1]
    third = (factor * COEFS[3]) * here
    total = (scale * v_ref[v_at] + scale * (-shift - 1.5 * COEFS[0])) * here
    for axis, size in ((1, NZ), (0, NY)):
        after, before = pltpu.roll(here, 1, axis), pltpu.roll(here, size - 1, axis)
        both = after + before
        even = third + (factor * EVEN) * both
        odd = (factor * ODD) * (after - before)
        near += both
        total += pltpu.roll(even + odd, 3, axis) + pltpu.roll(even - odd, size - 3, axis)
    total += (factor * COEFS[1]) * near
    for k in range(2, REACH + 1):
        total += (factor * COEFS[k]) * (src[orb, at + k] + src[orb, at - k])
    return total


def kernel(orbitals, potential, filtered, corr, ham,
           p0, p1, p2, p3, p4, hy, v_ref, every, acc, rows,
           in_sem, v_send, v_recv, a_send, a_recv, b_send, b_recv, c_send, c_recv,
           x_send, x_recv, out_sem, r_send, r_recv, met):
    g = lax.axis_index("grid")
    o = lax.axis_index("orb")
    x_lo, z, y = g // 32, (g // 4) % 8, g % 4
    up = (lax.rem(g + 1, 64), o)
    down = (lax.rem(g + 63, 64), o)
    o_core = o + 1 - 2 * lax.rem(o, 2)
    o_far = lax.rem(o + 2, 4)
    core = (g, o_core)
    far = (g, o_far)
    corner_up = (z == 7) & (y == 3) & (lax.rem(o, 2) == 1)
    corner_down = (z == 0) & (y == 0) & (lax.rem(o, 2) == 1)
    corner = corner_up | corner_down
    across = (lax.rem(g + 32, 64), o)
    onward = (x_lo * 32 + jnp.where(corner_up, 0, 31), o)
    up_first = (jnp.where(corner_up, across[0], up[0]), o)
    down_first = (jnp.where(corner_down, across[0], down[0]), o)
    up_at, up_sem = jnp.where(corner_up, 3 * OWN, 0), jnp.where(corner_up, 2, 0)
    down_at, down_sem = jnp.where(corner_down, 3 * OWN, 2 * OWN), jnp.where(corner_down, 2, 1)
    onward_at, onward_sem = jnp.where(corner_up, 0, 2 * OWN), jnp.where(corner_up, 0, 1)

    offsets = [(dx, dz, dy) for dx in range(2) for dz in range(8) for dy in range(4) if dx or dz or dy]
    offsets.sort(key=lambda d: -(d[0] + min(d[1], 8 - d[1]) + min(d[2], 4 - d[2])))
    others = [(lax.rem(x_lo + dx, 2) * 32 + lax.rem(z + dz, 8) * 4 + lax.rem(y + dy, 4), o) for dx, dz, dy in offsets]

    barrier = pltpu.get_barrier_semaphore()
    beside = [(x_lo * 32 + lax.rem(z + d, 8) * 4 + y, o) for d in (1, 7)]
    partners = [up, down, across] + beside + [core, far]
    for partner in partners:
        pl.semaphore_signal(barrier, inc=1, device_id=partner, device_id_type=MESH)

    def along_z(d):
        return (x_lo * 32 + lax.rem(z + d, 8) * 4 + y, o)

    rounds = [beside, [along_z(2), along_z(6)], [along_z(4)], [up, down], [across]]

    def greet(n):
        for partner in rounds[n]:
            pl.semaphore_signal(met.at[n], inc=1, device_id=partner, device_id_type=MESH)

    def heard(n):
        pl.semaphore_wait(met.at[n], len(rounds[n]))

    own_v = pltpu.make_async_copy(potential, v_ref.at[pl.ds(REACH, OWN)], in_sem.at[4])
    own_v.start()
    own_in = [pltpu.make_async_copy(orbitals.at[i], p0.at[i, pl.ds(OWN, OWN)], in_sem.at[i]) for i in range(4)]
    for copy in own_in:
        copy.start()

    pl.semaphore_wait(barrier, len(partners))

    def remote(src, dst, send, recv, device):
        return pltpu.make_async_remote_copy(
            src_ref=src, dst_ref=dst, send_sem=send, recv_sem=recv, device_id=device, device_id_type=MESH
        )

    half = REACH // 2
    part = half * lax.rem(o, 2)
    above = v_ref.at[pl.ds(part, half)]
    below = v_ref.at[pl.ds(REACH + OWN + part, half)]
    v_copies = [
        remote(potential.at[pl.ds(OWN - REACH + part, half)], above, v_send.at[0], v_recv.at[0], up),
        remote(potential.at[pl.ds(part, half)], below, v_send.at[1], v_recv.at[1], down),
    ]
    v_shared = [
        remote(above, above, v_send.at[2], v_recv.at[2], core),
        remote(below, below, v_send.at[3], v_recv.at[3], core),
    ]

    def block_copies(i, src, dst, send, recv):
        return [
            remote(src, dst.at[i, pl.ds(up_at, OWN)], send.at[i, 0], recv.at[i, up_sem], up_first),
            remote(src, dst.at[i, pl.ds(down_at, OWN)], send.at[i, 1], recv.at[i, down_sem], down_first),
        ]

    def block_arrivals(i, dst, send, recv):
        return [
            remote(dst.at[i, pl.ds(0, OWN)], dst.at[i, pl.ds(0, OWN)], send.at[i, 0], recv.at[i, 0], up),
            remote(dst.at[i, pl.ds(2 * OWN, OWN)], dst.at[i, pl.ds(2 * OWN, OWN)], send.at[i, 1], recv.at[i, 1], down),
        ]

    def corner_copy(i, dst, send, recv):
        return remote(
            dst.at[i, pl.ds(3 * OWN, OWN)], dst.at[i, pl.ds(onward_at, OWN)],
            send.at[i, 2], recv.at[i, onward_sem], onward,
        )

    def send_onward(i, dst, send, recv):
        @pl.when(corner)
        def _():
            remote(
                dst.at[i, pl.ds(3 * OWN, OWN)], dst.at[i, pl.ds(3 * OWN, OWN)], send.at[i, 2], recv.at[i, 2], across
            ).wait_recv()
            corner_copy(i, dst, send, recv).start()

    a_copies = [block_copies(i, orbitals.at[i], p0, a_send, a_recv) for i in range(4)]
    a_arrivals = [block_arrivals(i, p0, a_send, a_recv) for i in range(4)]
    b_copies = [block_copies(i, p2.at[i, pl.ds(OWN, OWN)], p2, b_send, b_recv) for i in range(4)]
    b_arrivals = [block_arrivals(i, p2, b_send, b_recv) for i in range(4)]
    c_copies = [
        [
            remote(p4.at[i, pl.ds(OWN, REACH)], p4.at[i, pl.ds(0, REACH)], c_send.at[i, 0], c_recv.at[i, 0], up),
            remote(p4.at[i, pl.ds(REACH, REACH)], p4.at[i, pl.ds(REACH + OWN, REACH)], c_send.at[i, 1], c_recv.at[i, 1], down),
        ]
        for i in range(4)
    ]
    x_copies = [
        [
            remote(every.at[o, i], every.at[o, i], x_send.at[i, 0], x_recv.at[i, 0], core),
            remote(every.at[o, i], every.at[o, i], x_send.at[i, 1], x_recv.at[i, 1], far),
            remote(every.at[o_far, i], every.at[o_far, i], x_send.at[i, 2], x_recv.at[i, 2], core),
        ]
        for i in range(4)
    ]
    out_copies = [pltpu.make_async_copy(every.at[o, i], filtered.at[i], out_sem.at[i]) for i in range(4)]

    def start(copies):
        for copy in copies:
            copy.start()

    def arrived(copies):
        for copy in copies:
            copy.wait_recv()

    gone = []

    def sent(copies):
        for copy in copies:
            copy.wait_send()
        gone.append(copies)

    def layers(count, body):
        def step(at, carry):
            body(at)
            return carry
        lax.fori_loop(0, count, step, 0, unroll=8)

    def unit_a(i):
        if i == 0:
            own_v.wait()
            arrived(v_copies)
            start(v_shared)
        own_in[i].wait()
        arrived(a_arrivals[i])
        if i == 0:
            arrived(v_shared)

        def first(at):
            p1[i, at] = stencil_layer(p0, i, at + REACH, v_ref, at, FACTORS[0][0], CENTRE)
        layers(2 * OWN, first)

        def second(at):
            p2[i, at + OWN] = stencil_layer(
                p1, i, at + REACH, v_ref, at + REACH, FACTORS[1][0], CENTRE
            ) - FACTORS[1][1] * p0[i, at + OWN]
        layers(OWN, second)

    def unit_b(i):
        arrived(b_arrivals[i])

        def third(at):
            p3[i, at] = stencil_layer(
                p2, i, at + REACH, v_ref, at, FACTORS[2][0], CENTRE
            ) - FACTORS[2][1] * p1[i, at]
        layers(2 * OWN, third)

        def fourth(at):
            value = stencil_layer(
                p3, i, at + REACH, v_ref, at + REACH, FACTORS[3][0], CENTRE
            ) - FACTORS[3][1] * p2[i, at + OWN]
            p4[i, at + REACH] = value
            every[o, i, at] = value
        layers(OWN, fourth)
        x_copies[i][1].start()
        x_copies[i][0].start()
        out_copies[i].start()

    def unit_c(i):
        arrived(c_copies[i])

        def applied(at):
            hy[i, at] = stencil_layer(p4, i, at + REACH, v_ref, at + REACH, 1.0, 0.0)
        layers(OWN, applied)

    def pass_on(i):
        x_copies[i][1].wait_recv()
        x_copies[i][2].start()

    def products(fields, partners_of):
        def step(at, sums):
            sums = list(sums)
            for part in range(NY // 8):
                rows = pl.ds(part * 8, 8)
                left = [hy[i, at, rows, :] if kind else every[o, i, at, rows, :] for kind, i in fields]
                for n, (slot, j) in enumerate(partners_of):
                    right = every[slot, j, at, rows, :]
                    for m in range(len(fields)):
                        sums[m * len(partners_of) + n] += left[m] * right
            return tuple(sums)

        zero = jnp.zeros((8, NZ), jnp.float32)
        sums = lax.fori_loop(0, OWN, step, (zero,) * (len(fields) * len(partners_of)))
        for m, (kind, i) in enumerate(fields):
            for n, (slot, j) in enumerate(partners_of):
                value = jnp.sum(sums[m * len(partners_of) + n], axis=0, keepdims=True)
                acc[pl.ds((kind * 4 + i) * 16 + slot * 4 + j, 1), :] = value

    def unit_d(i, slots):
        products([(0, i), (1, i)], [(slot, j) for slot in slots for j in range(i + 1)])
        if i:
            products([(kind, m) for kind in range(2) for m in range(i)], [(slot, i) for slot in slots])

    def unit_n(i):
        x_copies[i][0].wait_recv()
        unit_d(i, (o, o_core))

    def unit_f(i):
        x_copies[i][2].wait_recv()
        unit_d(i, (o_far, lax.rem(o_core + 2, 4)))

    start(a_copies[0])
    start(v_copies)
    greet(0)
    start(a_copies[1])
    start(a_copies[2])
    start(a_copies[3])
    send_onward(0, p0, a_send, a_recv)
    send_onward(1, p0, a_send, a_recv)
    heard(0)
    greet(1)
    send_onward(2, p0, a_send, a_recv)
    send_onward(3, p0, a_send, a_recv)
    unit_a(0)
    start(b_copies[0])
    heard(1)
    greet(2)
    unit_a(1)
    start(b_copies[1])
    send_onward(0, p2, b_send, b_recv)
    heard(2)
    greet(3)
    unit_a(2)
    start(b_copies[2])
    send_onward(1, p2, b_send, b_recv)
    unit_a(3)
    start(b_copies[3])
    send_onward(2, p2, b_send, b_recv)
    heard(3)
    greet(4)
    unit_b(0)
    start(c_copies[0])
    send_onward(3, p2, b_send, b_recv)
    unit_b(1)
    start(c_copies[1])
    unit_b(2)
    start(c_copies[2])
    heard(4)
    unit_b(3)
    start(c_copies[3])
    unit_c(0)
    pass_on(0)
    unit_c(1)
    pass_on(1)
    unit_n(0)
    unit_n(1)
    unit_c(2)
    pass_on(2)
    unit_n(2)
    unit_f(0)
    unit_f(1)
    unit_f(2)
    unit_c(3)
    pass_on(3)
    unit_n(3)
    unit_f(3)

    flat = lax.dot_general(
        jnp.full((8, NZ), 1.0 / (512 * NY * NZ), jnp.float32), acc[...], (((1,), (1,)), ((), ())),
        precision=lax.Precision.HIGHEST, preferred_element_type=jnp.float32,
    )
    rows[pl.ds(g, 1)] = flat[0:1]
    sum_copies = [
        remote(rows.at[pl.ds(g, 1)], rows.at[pl.ds(g, 1)], r_send.at[n], r_recv.at[n], peer)
        for n, peer in enumerate(others)
    ]
    start(sum_copies)
    arrived(sum_copies)
    total = jnp.sum(rows[...], axis=0, keepdims=True)
    for kind, ref in ((0, corr), (1, ham)):
        for i in range(4):
            first = (kind * 4 + i) * 16
            ref[pl.ds(i, 1), :] = total[:, first : first + 16]

    for copies in [v_copies, v_shared, sum_copies] + a_copies + b_copies + c_copies + x_copies:
        if not any(copies is other for other in gone):
            sent(copies)
    for copy in out_copies:
        copy.wait()

    @pl.when(corner)
    def _():
        for i in range(4):
            corner_copy(i, p0, a_send, a_recv).wait_send()
            corner_copy(i, p2, b_send, b_recv).wait_send()


def per_device(orbitals, potential):
    dma = pltpu.SemaphoreType.DMA
    field = lambda count: pltpu.VMEM((4, count, NY, NZ), jnp.float32)
    return pl.pallas_call(
        kernel,
        out_shape=(
            jax.ShapeDtypeStruct((4, OWN, NY, NZ), jnp.float32),
            jax.ShapeDtypeStruct((4, 16), jnp.float32),
            jax.ShapeDtypeStruct((4, 16), jnp.float32),
        ),
        in_specs=[pl.BlockSpec(memory_space=pltpu.HBM)] * 2,
        out_specs=(
            pl.BlockSpec(memory_space=pl.ANY),
            pl.BlockSpec(memory_space=pltpu.VMEM),
            pl.BlockSpec(memory_space=pltpu.VMEM),
        ),
        scratch_shapes=[
            field(4 * OWN), field(2 * OWN), field(4 * OWN), field(2 * OWN), field(2 * OWN), field(OWN),
            pltpu.VMEM((2 * OWN, NY, NZ), jnp.float32),
            pltpu.VMEM((4, 4, OWN, NY, NZ), jnp.float32),
            pltpu.VMEM((128, NZ), jnp.float32),
            pltpu.VMEM((64, NZ), jnp.float32),
            dma((5,)), dma((4,)), dma((4,)),
            dma((4, 3)), dma((4, 3)), dma((4, 3)), dma((4, 3)), dma((4, 2)), dma((4, 2)),
            dma((4, 3)), dma((4, 3)), dma((4,)),
            dma((63,)), dma((63,)), pltpu.SemaphoreType.REGULAR((5,)),
        ],
        compiler_params=pltpu.CompilerParams(
            collective_id=0, has_side_effects=True, vmem_limit_bytes=40 * 1024 * 1024
        ),
    )(orbitals, potential)


def solution(mesh):
    return jax.shard_map(
        per_device,
        mesh=mesh,
        in_specs=(P("orb", "grid", None, None), P("grid", None, None)),
        out_specs=(P("orb", "grid", None, None), P("orb", None), P("orb", None)),
        check_vma=False,
    )
```

```python
import jax
import jax.numpy as jnp
from jax import lax
from jax.experimental import pallas as pl
from jax.experimental.pallas import tpu as pltpu
from jax.sharding import PartitionSpec as P

COEFS = (-205.0 / 72.0, 8.0 / 5.0, -1.0 / 5.0, 8.0 / 315.0, -1.0 / 560.0)
LOWER = -1.0
CUT = 4.0
UPPER = 10.0

HALF = (UPPER - CUT) / 2.0
CENTRE = (UPPER + CUT) / 2.0
SIGMA_1 = HALF / (LOWER - CENTRE)


def chebyshev_factors():
    factors = [(SIGMA_1 / HALF, 0.0)]
    sigma = SIGMA_1
    for _ in range(3):
        sigma_new = 1.0 / (2.0 / SIGMA_1 - sigma)
        factors.append((2.0 * sigma_new / HALF, sigma * sigma_new))
        sigma = sigma_new
    return factors


FACTORS = chebyshev_factors()
REACH = 4
OWN = 8
NY = 32
NZ = 128
MESH = pl.DeviceIdType.MESH


EVEN = (COEFS[2] + COEFS[4]) / 2.0
ODD = (COEFS[4] - COEFS[2]) / 2.0


def stencil_layer(src, orb, at, v_ref, v_at, scale, shift):
    here = src[orb, at]
    factor = -0.5 * scale
    near = src[orb, at + 1] + src[orb, at - 1]
    third = (factor * COEFS[3]) * here
    total = (scale * v_ref[v_at] + scale * (-shift - 1.5 * COEFS[0])) * here
    for axis, size in ((1, NZ), (0, NY)):
        after, before = pltpu.roll(here, 1, axis), pltpu.roll(here, size - 1, axis)
        both = after + before
        even = third + (factor * EVEN) * both
        odd = (factor * ODD) * (after - before)
        near += both
        total += pltpu.roll(even + odd, 3, axis) + pltpu.roll(even - odd, size - 3, axis)
    total += (factor * COEFS[1]) * near
    for k in range(2, REACH + 1):
        total += (factor * COEFS[k]) * (src[orb, at + k] + src[orb, at - k])
    return total


def kernel(orbitals, potential, filtered, corr, ham,
           p0, p1, p2, p3, p4, hy, v_ref, every, acc, rows,
           in_sem, v_send, v_recv, a_send, a_recv, b_send, b_recv, c_send, c_recv,
           x_send, x_recv, out_sem, r_send, r_recv, met):
    g = lax.axis_index("grid")
    o = lax.axis_index("orb")
    x_lo, z, y = g // 32, (g // 4) % 8, g % 4
    up = (lax.rem(g + 1, 64), o)
    down = (lax.rem(g + 63, 64), o)
    o_core = o + 1 - 2 * lax.rem(o, 2)
    o_far = lax.rem(o + 2, 4)
    core = (g, o_core)
    far = (g, o_far)
    corner_up = (z == 7) & (y == 3) & (lax.rem(o, 2) == 1)
    corner_down = (z == 0) & (y == 0) & (lax.rem(o, 2) == 1)
    corner = corner_up | corner_down
    across = (lax.rem(g + 32, 64), o)
    onward = (x_lo * 32 + jnp.where(corner_up, 0, 31), o)
    up_first = (jnp.where(corner_up, across[0], up[0]), o)
    down_first = (jnp.where(corner_down, across[0], down[0]), o)
    up_at, up_sem = jnp.where(corner_up, 3 * OWN, 0), jnp.where(corner_up, 2, 0)
    down_at, down_sem = jnp.where(corner_down, 3 * OWN, 2 * OWN), jnp.where(corner_down, 2, 1)
    onward_at, onward_sem = jnp.where(corner_up, 0, 2 * OWN), jnp.where(corner_up, 0, 1)

    offsets = [(dx, dz, dy) for dx in range(2) for dz in range(8) for dy in range(4) if dx or dz or dy]
    offsets.sort(key=lambda d: -(d[0] + min(d[1], 8 - d[1]) + min(d[2], 4 - d[2])))
    others = [(lax.rem(x_lo + dx, 2) * 32 + lax.rem(z + dz, 8) * 4 + lax.rem(y + dy, 4), o) for dx, dz, dy in offsets]

    barrier = pltpu.get_barrier_semaphore()
    beside = [(x_lo * 32 + lax.rem(z + d, 8) * 4 + y, o) for d in (1, 7)]
    partners = [up, down, across] + beside + [core, far]
    for partner in partners:
        pl.semaphore_signal(barrier, inc=1, device_id=partner, device_id_type=MESH)

    def along_z(d):
        return (x_lo * 32 + lax.rem(z + d, 8) * 4 + y, o)

    rounds = [beside, [along_z(2), along_z(6)], [along_z(4)], [up, down], [across]]

    def greet(n):
        for partner in rounds[n]:
            pl.semaphore_signal(met.at[n], inc=1, device_id=partner, device_id_type=MESH)

    def heard(n):
        pl.semaphore_wait(met.at[n], len(rounds[n]))

    own_v = pltpu.make_async_copy(potential, v_ref.at[pl.ds(REACH, OWN)], in_sem.at[4])
    own_v.start()
    own_in = [pltpu.make_async_copy(orbitals.at[i], p0.at[i, pl.ds(OWN, OWN)], in_sem.at[i]) for i in range(4)]
    for copy in own_in:
        copy.start()

    pl.semaphore_wait(barrier, len(partners))

    def remote(src, dst, send, recv, device):
        return pltpu.make_async_remote_copy(
            src_ref=src, dst_ref=dst, send_sem=send, recv_sem=recv, device_id=device, device_id_type=MESH
        )

    half = REACH // 2
    part = half * lax.rem(o, 2)
    above = v_ref.at[pl.ds(part, half)]
    below = v_ref.at[pl.ds(REACH + OWN + part, half)]
    v_copies = [
        remote(potential.at[pl.ds(OWN - REACH + part, half)], above, v_send.at[0], v_recv.at[0], up),
        remote(potential.at[pl.ds(part, half)], below, v_send.at[1], v_recv.at[1], down),
    ]
    v_shared = [
        remote(above, above, v_send.at[2], v_recv.at[2], core),
        remote(below, below, v_send.at[3], v_recv.at[3], core),
    ]

    def block_copies(i, src, dst, send, recv):
        return [
            remote(src, dst.at[i, pl.ds(up_at, OWN)], send.at[i, 0], recv.at[i, up_sem], up_first),
            remote(src, dst.at[i, pl.ds(down_at, OWN)], send.at[i, 1], recv.at[i, down_sem], down_first),
        ]

    def block_arrivals(i, dst, send, recv):
        return [
            remote(dst.at[i, pl.ds(0, OWN)], dst.at[i, pl.ds(0, OWN)], send.at[i, 0], recv.at[i, 0], up),
            remote(dst.at[i, pl.ds(2 * OWN, OWN)], dst.at[i, pl.ds(2 * OWN, OWN)], send.at[i, 1], recv.at[i, 1], down),
        ]

    def corner_copy(i, dst, send, recv):
        return remote(
            dst.at[i, pl.ds(3 * OWN, OWN)], dst.at[i, pl.ds(onward_at, OWN)],
            send.at[i, 2], recv.at[i, onward_sem], onward,
        )

    def send_onward(i, dst, send, recv):
        @pl.when(corner)
        def _():
            remote(
                dst.at[i, pl.ds(3 * OWN, OWN)], dst.at[i, pl.ds(3 * OWN, OWN)], send.at[i, 2], recv.at[i, 2], across
            ).wait_recv()
            corner_copy(i, dst, send, recv).start()

    a_copies = [block_copies(i, orbitals.at[i], p0, a_send, a_recv) for i in range(4)]
    a_arrivals = [block_arrivals(i, p0, a_send, a_recv) for i in range(4)]
    b_copies = [block_copies(i, p2.at[i, pl.ds(OWN, OWN)], p2, b_send, b_recv) for i in range(4)]
    b_arrivals = [block_arrivals(i, p2, b_send, b_recv) for i in range(4)]
    c_copies = [
        [
            remote(p4.at[i, pl.ds(OWN, REACH)], p4.at[i, pl.ds(0, REACH)], c_send.at[i, 0], c_recv.at[i, 0], up),
            remote(p4.at[i, pl.ds(REACH, REACH)], p4.at[i, pl.ds(REACH + OWN, REACH)], c_send.at[i, 1], c_recv.at[i, 1], down),
        ]
        for i in range(4)
    ]
    x_copies = [
        [
            remote(every.at[o, i], every.at[o, i], x_send.at[i, 0], x_recv.at[i, 0], core),
            remote(every.at[o, i], every.at[o, i], x_send.at[i, 1], x_recv.at[i, 1], far),
            remote(every.at[o_far, i], every.at[o_far, i], x_send.at[i, 2], x_recv.at[i, 2], core),
        ]
        for i in range(4)
    ]
    out_copies = [pltpu.make_async_copy(every.at[o, i], filtered.at[i], out_sem.at[i]) for i in range(4)]

    def start(copies):
        for copy in copies:
            copy.start()

    def arrived(copies):
        for copy in copies:
            copy.wait_recv()

    gone = []

    def sent(copies):
        for copy in copies:
            copy.wait_send()
        gone.append(copies)

    def layers(count, body):
        def step(at, carry):
            body(at)
            return carry
        lax.fori_loop(0, count, step, 0, unroll=8)

    def unit_a(i):
        if i == 0:
            own_v.wait()
            arrived(v_copies)
            start(v_shared)
        own_in[i].wait()
        arrived(a_arrivals[i])
        if i == 0:
            arrived(v_shared)

        def first(at):
            p1[i, at] = stencil_layer(p0, i, at + REACH, v_ref, at, FACTORS[0][0], CENTRE)
        layers(2 * OWN, first)

        def second(at):
            p2[i, at + OWN] = stencil_layer(
                p1, i, at + REACH, v_ref, at + REACH, FACTORS[1][0], CENTRE
            ) - FACTORS[1][1] * p0[i, at + OWN]
        layers(OWN, second)

    def unit_b(i):
        arrived(b_arrivals[i])

        def third(at):
            p3[i, at] = stencil_layer(
                p2, i, at + REACH, v_ref, at, FACTORS[2][0], CENTRE
            ) - FACTORS[2][1] * p1[i, at]
        layers(2 * OWN, third)

        def fourth(at):
            value = stencil_layer(
                p3, i, at + REACH, v_ref, at + REACH, FACTORS[3][0], CENTRE
            ) - FACTORS[3][1] * p2[i, at + OWN]
            p4[i, at + REACH] = value
            every[o, i, at] = value
        layers(OWN, fourth)
        x_copies[i][1].start()
        x_copies[i][0].start()
        out_copies[i].start()

    def unit_c(i):
        arrived(c_copies[i])

        def applied(at):
            hy[i, at] = stencil_layer(p4, i, at + REACH, v_ref, at + REACH, 1.0, 0.0)
        layers(OWN, applied)

    def pass_on(i):
        x_copies[i][1].wait_recv()
        x_copies[i][2].start()

    def products(fields, partners_of):
        def step(at, sums):
            sums = list(sums)
            for part in range(NY // 8):
                rows = pl.ds(part * 8, 8)
                left = [hy[i, at, rows, :] if kind else every[o, i, at, rows, :] for kind, i in fields]
                for n, (slot, j) in enumerate(partners_of):
                    right = every[slot, j, at, rows, :]
                    for m in range(len(fields)):
                        sums[m * len(partners_of) + n] += left[m] * right
            return tuple(sums)

        zero = jnp.zeros((8, NZ), jnp.float32)
        sums = lax.fori_loop(0, OWN, step, (zero,) * (len(fields) * len(partners_of)))
        for m, (kind, i) in enumerate(fields):
            for n, (slot, j) in enumerate(partners_of):
                value = jnp.sum(sums[m * len(partners_of) + n], axis=0, keepdims=True)
                acc[pl.ds((kind * 4 + i) * 16 + slot * 4 + j, 1), :] = value

    def unit_d(i, slots):
        products([(0, i), (1, i)], [(slot, j) for slot in slots for j in range(i + 1)])
        if i:
            products([(kind, m) for kind in range(2) for m in range(i)], [(slot, i) for slot in slots])

    def unit_n(i):
        x_copies[i][0].wait_recv()
        unit_d(i, (o, o_core))

    def unit_f(i):
        x_copies[i][2].wait_recv()
        unit_d(i, (o_far, lax.rem(o_core + 2, 4)))

    start(a_copies[0])
    start(v_copies)
    greet(0)
    start(a_copies[1])
    start(a_copies[2])
    start(a_copies[3])
    send_onward(0, p0, a_send, a_recv)
    heard(0)
    greet(1)
    send_onward(1, p0, a_send, a_recv)
    unit_a(0)
    start(b_copies[0])
    send_onward(2, p0, a_send, a_recv)
    send_onward(3, p0, a_send, a_recv)
    heard(1)
    greet(2)
    unit_a(1)
    start(b_copies[1])
    send_onward(0, p2, b_send, b_recv)
    heard(2)
    greet(3)
    unit_a(2)
    start(b_copies[2])
    send_onward(1, p2, b_send, b_recv)
    unit_a(3)
    start(b_copies[3])
    send_onward(2, p2, b_send, b_recv)
    heard(3)
    greet(4)
    send_onward(3, p2, b_send, b_recv)
    unit_b(0)
    start(c_copies[0])
    unit_b(1)
    start(c_copies[1])
    unit_b(2)
    start(c_copies[2])
    heard(4)
    unit_b(3)
    start(c_copies[3])
    unit_c(0)
    pass_on(0)
    unit_c(1)
    pass_on(1)
    unit_n(0)
    unit_n(1)
    unit_c(2)
    pass_on(2)
    unit_n(2)
    unit_f(0)
    unit_f(1)
    unit_f(2)
    unit_c(3)
    pass_on(3)
    unit_n(3)
    unit_f(3)

    flat = lax.dot_general(
        jnp.full((8, NZ), 1.0 / (512 * NY * NZ), jnp.float32), acc[...], (((1,), (1,)), ((), ())),
        precision=lax.Precision.HIGHEST, preferred_element_type=jnp.float32,
    )
    rows[pl.ds(g, 1)] = flat[0:1]
    sum_copies = [
        remote(rows.at[pl.ds(g, 1)], rows.at[pl.ds(g, 1)], r_send.at[n], r_recv.at[n], peer)
        for n, peer in enumerate(others)
    ]
    start(sum_copies)
    arrived(sum_copies)
    total = jnp.sum(rows[...], axis=0, keepdims=True)
    for kind, ref in ((0, corr), (1, ham)):
        for i in range(4):
            first = (kind * 4 + i) * 16
            ref[pl.ds(i, 1), :] = total[:, first : first + 16]

    for copies in [v_copies, v_shared, sum_copies] + a_copies + b_copies + c_copies + x_copies:
        if not any(copies is other for other in gone):
            sent(copies)
    for copy in out_copies:
        copy.wait()

    @pl.when(corner)
    def _():
        for i in range(4):
            corner_copy(i, p0, a_send, a_recv).wait_send()
            corner_copy(i, p2, b_send, b_recv).wait_send()


def per_device(orbitals, potential):
    orbitals, potential = (pltpu.with_memory_space_constraint(value, pltpu.HBM) for value in (orbitals, potential))
    dma = pltpu.SemaphoreType.DMA
    field = lambda count: pltpu.VMEM((4, count, NY, NZ), jnp.float32)
    return pl.pallas_call(
        kernel,
        out_shape=(
            jax.ShapeDtypeStruct((4, OWN, NY, NZ), jnp.float32),
            jax.ShapeDtypeStruct((4, 16), jnp.float32),
            jax.ShapeDtypeStruct((4, 16), jnp.float32),
        ),
        in_specs=[pl.BlockSpec(memory_space=pltpu.HBM)] * 2,
        out_specs=(
            pl.BlockSpec(memory_space=pl.ANY),
            pl.BlockSpec(memory_space=pltpu.VMEM),
            pl.BlockSpec(memory_space=pltpu.VMEM),
        ),
        scratch_shapes=[
            field(4 * OWN), field(2 * OWN), field(4 * OWN), field(2 * OWN), field(2 * OWN), field(OWN),
            pltpu.VMEM((2 * OWN, NY, NZ), jnp.float32),
            pltpu.VMEM((4, 4, OWN, NY, NZ), jnp.float32),
            pltpu.VMEM((128, NZ), jnp.float32),
            pltpu.VMEM((64, NZ), jnp.float32),
            dma((5,)), dma((4,)), dma((4,)),
            dma((4, 3)), dma((4, 3)), dma((4, 3)), dma((4, 3)), dma((4, 2)), dma((4, 2)),
            dma((4, 3)), dma((4, 3)), dma((4,)),
            dma((63,)), dma((63,)), pltpu.SemaphoreType.REGULAR((5,)),
        ],
        compiler_params=pltpu.CompilerParams(
            collective_id=0, has_side_effects=True, vmem_limit_bytes=40 * 1024 * 1024
        ),
    )(orbitals, potential)


def solution(mesh):
    return jax.shard_map(
        per_device,
        mesh=mesh,
        in_specs=(P("orb", "grid", None, None), P("grid", None, None)),
        out_specs=(P("orb", "grid", None, None), P("orb", None), P("orb", None)),
        check_vma=False,
    )
```

```python
import jax
import jax.numpy as jnp
from jax import lax
from jax.experimental import pallas as pl
from jax.experimental.pallas import tpu as pltpu
from jax.sharding import PartitionSpec as P

COEFS = (-205.0 / 72.0, 8.0 / 5.0, -1.0 / 5.0, 8.0 / 315.0, -1.0 / 560.0)
LOWER = -1.0
CUT = 4.0
UPPER = 10.0

HALF = (UPPER - CUT) / 2.0
CENTRE = (UPPER + CUT) / 2.0
SIGMA_1 = HALF / (LOWER - CENTRE)


def chebyshev_factors():
    factors = [(SIGMA_1 / HALF, 0.0)]
    sigma = SIGMA_1
    for _ in range(3):
        sigma_new = 1.0 / (2.0 / SIGMA_1 - sigma)
        factors.append((2.0 * sigma_new / HALF, sigma * sigma_new))
        sigma = sigma_new
    return factors


FACTORS = chebyshev_factors()
REACH = 4
OWN = 8
NY = 32
NZ = 128
MESH = pl.DeviceIdType.MESH


EVEN = (COEFS[2] + COEFS[4]) / 2.0
ODD = (COEFS[4] - COEFS[2]) / 2.0


def stencil_layer(src, orb, at, v_ref, v_at, scale, shift):
    here = src[orb, at]
    factor = -0.5 * scale
    near = src[orb, at + 1] + src[orb, at - 1]
    third = (factor * COEFS[3]) * here
    total = (scale * v_ref[v_at] + scale * (-shift - 1.5 * COEFS[0])) * here
    for axis, size in ((1, NZ), (0, NY)):
        after, before = pltpu.roll(here, 1, axis), pltpu.roll(here, size - 1, axis)
        both = after + before
        even = third + (factor * EVEN) * both
        odd = (factor * ODD) * (after - before)
        near += both
        total += pltpu.roll(even + odd, 3, axis) + pltpu.roll(even - odd, size - 3, axis)
    total += (factor * COEFS[1]) * near
    for k in range(2, REACH + 1):
        total += (factor * COEFS[k]) * (src[orb, at + k] + src[orb, at - k])
    return total


def kernel(orbitals, potential, filtered, grams,
           p0, p1, p2, p3, p4, hy, v_ref, every, acc, rows,
           in_sem, v_send, v_recv, a_send, a_recv, b_send, b_recv, c_send, c_recv,
           x_send, x_recv, out_sem, r_send, r_recv, met):
    g = lax.axis_index("grid")
    o = lax.axis_index("orb")
    x_lo, z, y = g // 32, (g // 4) % 8, g % 4
    up = (lax.rem(g + 1, 64), o)
    down = (lax.rem(g + 63, 64), o)
    o_core = o + 1 - 2 * lax.rem(o, 2)
    o_far = lax.rem(o + 2, 4)
    core = (g, o_core)
    far = (g, o_far)
    corner_up = (z == 7) & (y == 3) & (lax.rem(o, 2) == 1)
    corner_down = (z == 0) & (y == 0) & (lax.rem(o, 2) == 1)
    corner = corner_up | corner_down
    across = (lax.rem(g + 32, 64), o)
    onward = (x_lo * 32 + jnp.where(corner_up, 0, 31), o)
    up_first = (jnp.where(corner_up, across[0], up[0]), o)
    down_first = (jnp.where(corner_down, across[0], down[0]), o)
    up_at, up_sem = jnp.where(corner_up, 3 * OWN, 0), jnp.where(corner_up, 2, 0)
    down_at, down_sem = jnp.where(corner_down, 3 * OWN, 2 * OWN), jnp.where(corner_down, 2, 1)
    onward_at, onward_sem = jnp.where(corner_up, 0, 2 * OWN), jnp.where(corner_up, 0, 1)

    offsets = [(dx, dz, dy) for dx in range(2) for dz in range(8) for dy in range(4) if dx or dz or dy]
    offsets.sort(key=lambda d: -(d[0] + min(d[1], 8 - d[1]) + min(d[2], 4 - d[2])))
    others = [(lax.rem(x_lo + dx, 2) * 32 + lax.rem(z + dz, 8) * 4 + lax.rem(y + dy, 4), o) for dx, dz, dy in offsets]

    barrier = pltpu.get_barrier_semaphore()
    beside = [(x_lo * 32 + lax.rem(z + d, 8) * 4 + y, o) for d in (1, 7)]
    partners = [up, down, across] + beside + [core, far]
    for partner in partners:
        pl.semaphore_signal(barrier, inc=1, device_id=partner, device_id_type=MESH)

    def along_z(d):
        return (x_lo * 32 + lax.rem(z + d, 8) * 4 + y, o)

    rounds = [beside, [along_z(2), along_z(6)], [along_z(4)], [up, down], [across]]

    def greet(n):
        for partner in rounds[n]:
            pl.semaphore_signal(met.at[n], inc=1, device_id=partner, device_id_type=MESH)

    def heard(n):
        pl.semaphore_wait(met.at[n], len(rounds[n]))

    own_v = pltpu.make_async_copy(potential, v_ref.at[pl.ds(REACH, OWN)], in_sem.at[4])
    own_v.start()
    own_in = [pltpu.make_async_copy(orbitals.at[i], p0.at[i, pl.ds(OWN, OWN)], in_sem.at[i]) for i in range(4)]
    for copy in own_in:
        copy.start()

    pl.semaphore_wait(barrier, len(partners))

    def remote(src, dst, send, recv, device):
        return pltpu.make_async_remote_copy(
            src_ref=src, dst_ref=dst, send_sem=send, recv_sem=recv, device_id=device, device_id_type=MESH
        )

    half = REACH // 2
    part = half * lax.rem(o, 2)
    above = v_ref.at[pl.ds(part, half)]
    below = v_ref.at[pl.ds(REACH + OWN + part, half)]
    v_copies = [
        remote(potential.at[pl.ds(OWN - REACH + part, half)], above, v_send.at[0], v_recv.at[0], up),
        remote(potential.at[pl.ds(part, half)], below, v_send.at[1], v_recv.at[1], down),
    ]
    v_shared = [
        remote(above, above, v_send.at[2], v_recv.at[2], core),
        remote(below, below, v_send.at[3], v_recv.at[3], core),
    ]

    def block_copies(i, src, dst, send, recv):
        return [
            remote(src, dst.at[i, pl.ds(up_at, OWN)], send.at[i, 0], recv.at[i, up_sem], up_first),
            remote(src, dst.at[i, pl.ds(down_at, OWN)], send.at[i, 1], recv.at[i, down_sem], down_first),
        ]

    def block_arrivals(i, dst, send, recv):
        return [
            remote(dst.at[i, pl.ds(0, OWN)], dst.at[i, pl.ds(0, OWN)], send.at[i, 0], recv.at[i, 0], up),
            remote(dst.at[i, pl.ds(2 * OWN, OWN)], dst.at[i, pl.ds(2 * OWN, OWN)], send.at[i, 1], recv.at[i, 1], down),
        ]

    def corner_copy(i, dst, send, recv):
        return remote(
            dst.at[i, pl.ds(3 * OWN, OWN)], dst.at[i, pl.ds(onward_at, OWN)],
            send.at[i, 2], recv.at[i, onward_sem], onward,
        )

    def send_onward(i, dst, send, recv):
        @pl.when(corner)
        def _():
            remote(
                dst.at[i, pl.ds(3 * OWN, OWN)], dst.at[i, pl.ds(3 * OWN, OWN)], send.at[i, 2], recv.at[i, 2], across
            ).wait_recv()
            corner_copy(i, dst, send, recv).start()

    a_copies = [block_copies(i, orbitals.at[i], p0, a_send, a_recv) for i in range(4)]
    a_arrivals = [block_arrivals(i, p0, a_send, a_recv) for i in range(4)]
    b_copies = [block_copies(i, p2.at[i, pl.ds(OWN, OWN)], p2, b_send, b_recv) for i in range(4)]
    b_arrivals = [block_arrivals(i, p2, b_send, b_recv) for i in range(4)]
    c_copies = [
        [
            remote(p4.at[i, pl.ds(OWN, REACH)], p4.at[i, pl.ds(0, REACH)], c_send.at[i, 0], c_recv.at[i, 0], up),
            remote(p4.at[i, pl.ds(REACH, REACH)], p4.at[i, pl.ds(REACH + OWN, REACH)], c_send.at[i, 1], c_recv.at[i, 1], down),
        ]
        for i in range(4)
    ]
    x_copies = [
        [
            remote(every.at[o, i], every.at[o, i], x_send.at[i, 0], x_recv.at[i, 0], core),
            remote(every.at[o, i], every.at[o, i], x_send.at[i, 1], x_recv.at[i, 1], far),
            remote(every.at[o_far, i], every.at[o_far, i], x_send.at[i, 2], x_recv.at[i, 2], core),
        ]
        for i in range(4)
    ]
    out_copies = [pltpu.make_async_copy(every.at[o, i], filtered.at[i], out_sem.at[i]) for i in range(4)]

    def start(copies):
        for copy in copies:
            copy.start()

    def arrived(copies):
        for copy in copies:
            copy.wait_recv()

    gone = []

    def sent(copies):
        for copy in copies:
            copy.wait_send()
        gone.append(copies)

    def layers(count, body):
        def step(at, carry):
            body(at)
            return carry
        lax.fori_loop(0, count, step, 0, unroll=8)

    def unit_a(i):
        if i == 0:
            own_v.wait()
            arrived(v_copies)
            start(v_shared)
        own_in[i].wait()
        arrived(a_arrivals[i])
        if i == 0:
            arrived(v_shared)

        def first(at):
            p1[i, at] = stencil_layer(p0, i, at + REACH, v_ref, at, FACTORS[0][0], CENTRE)
        layers(2 * OWN, first)

        def second(at):
            p2[i, at + OWN] = stencil_layer(
                p1, i, at + REACH, v_ref, at + REACH, FACTORS[1][0], CENTRE
            ) - FACTORS[1][1] * p0[i, at + OWN]
        layers(OWN, second)

    def unit_b(i):
        arrived(b_arrivals[i])

        def third(at):
            p3[i, at] = stencil_layer(
                p2, i, at + REACH, v_ref, at, FACTORS[2][0], CENTRE
            ) - FACTORS[2][1] * p1[i, at]
        layers(2 * OWN, third)

        def fourth(at):
            value = stencil_layer(
                p3, i, at + REACH, v_ref, at + REACH, FACTORS[3][0], CENTRE
            ) - FACTORS[3][1] * p2[i, at + OWN]
            p4[i, at + REACH] = value
            every[o, i, at] = value
        layers(OWN, fourth)
        x_copies[i][1].start()
        x_copies[i][0].start()
        out_copies[i].start()

    def unit_c(i):
        arrived(c_copies[i])

        def applied(at):
            hy[i, at] = stencil_layer(p4, i, at + REACH, v_ref, at + REACH, 1.0, 0.0)
        layers(OWN, applied)

    def pass_on(i):
        x_copies[i][1].wait_recv()
        x_copies[i][2].start()

    def products(fields, partners_of):
        def step(at, sums):
            sums = list(sums)
            for part in range(NY // 8):
                rows = pl.ds(part * 8, 8)
                left = [hy[i, at, rows, :] if kind else every[o, i, at, rows, :] for kind, i in fields]
                for n, (slot, j) in enumerate(partners_of):
                    right = every[slot, j, at, rows, :]
                    for m in range(len(fields)):
                        sums[m * len(partners_of) + n] += left[m] * right
            return tuple(sums)

        zero = jnp.zeros((8, NZ), jnp.float32)
        sums = lax.fori_loop(0, OWN, step, (zero,) * (len(fields) * len(partners_of)))
        for m, (kind, i) in enumerate(fields):
            for n, (slot, j) in enumerate(partners_of):
                value = jnp.sum(sums[m * len(partners_of) + n], axis=0, keepdims=True)
                acc[pl.ds((kind * 4 + i) * 16 + slot * 4 + j, 1), :] = value

    def unit_d(i, slots):
        products([(0, i), (1, i)], [(slot, j) for slot in slots for j in range(i + 1)])
        if i:
            products([(kind, m) for kind in range(2) for m in range(i)], [(slot, i) for slot in slots])

    def unit_n(i):
        x_copies[i][0].wait_recv()
        unit_d(i, (o, o_core))

    def unit_f(i):
        x_copies[i][2].wait_recv()
        unit_d(i, (o_far, lax.rem(o_core + 2, 4)))

    start(a_copies[0])
    start(v_copies)
    greet(0)
    start(a_copies[1])
    start(a_copies[2])
    start(a_copies[3])
    send_onward(0, p0, a_send, a_recv)
    heard(0)
    greet(1)
    send_onward(1, p0, a_send, a_recv)
    unit_a(0)
    start(b_copies[0])
    send_onward(2, p0, a_send, a_recv)
    send_onward(3, p0, a_send, a_recv)
    heard(1)
    greet(2)
    unit_a(1)
    start(b_copies[1])
    send_onward(0, p2, b_send, b_recv)
    heard(2)
    greet(3)
    unit_a(2)
    start(b_copies[2])
    send_onward(1, p2, b_send, b_recv)
    unit_a(3)
    start(b_copies[3])
    send_onward(2, p2, b_send, b_recv)
    heard(3)
    greet(4)
    send_onward(3, p2, b_send, b_recv)
    unit_b(0)
    start(c_copies[0])
    unit_b(1)
    start(c_copies[1])
    unit_b(2)
    start(c_copies[2])
    heard(4)
    unit_b(3)
    start(c_copies[3])
    unit_c(0)
    pass_on(0)
    unit_c(1)
    pass_on(1)
    unit_n(0)
    unit_n(1)
    unit_c(2)
    pass_on(2)
    unit_n(2)
    unit_f(0)
    unit_f(1)
    unit_f(2)
    unit_c(3)
    pass_on(3)
    unit_n(3)
    unit_f(3)

    flat = lax.dot_general(
        jnp.full((8, NZ), 1.0 / (512 * NY * NZ), jnp.float32), acc[...], (((1,), (1,)), ((), ())),
        precision=lax.Precision.HIGHEST, preferred_element_type=jnp.float32,
    )
    rows[pl.ds(g, 1)] = flat[0:1]
    sum_copies = [
        remote(rows.at[pl.ds(g, 1)], rows.at[pl.ds(g, 1)], r_send.at[n], r_recv.at[n], peer)
        for n, peer in enumerate(others)
    ]
    start(sum_copies)
    arrived(sum_copies)
    total = jnp.sum(rows[...], axis=0, keepdims=True)
    for i in range(8):
        grams[pl.ds(i, 1), :] = total[:, 16 * i : 16 * i + 16]

    for copies in [v_copies, v_shared, sum_copies] + a_copies + b_copies + c_copies + x_copies:
        if not any(copies is other for other in gone):
            sent(copies)
    for copy in out_copies:
        copy.wait()

    @pl.when(corner)
    def _():
        for i in range(4):
            corner_copy(i, p0, a_send, a_recv).wait_send()
            corner_copy(i, p2, b_send, b_recv).wait_send()


def per_device(orbitals, potential):
    orbitals, potential = (pltpu.with_memory_space_constraint(value, pltpu.HBM) for value in (orbitals, potential))
    dma = pltpu.SemaphoreType.DMA
    field = lambda count: pltpu.VMEM((4, count, NY, NZ), jnp.float32)
    filtered, grams = pl.pallas_call(
        kernel,
        out_shape=(
            jax.ShapeDtypeStruct((4, OWN, NY, NZ), jnp.float32),
            jax.ShapeDtypeStruct((8, 16), jnp.float32),
        ),
        in_specs=[pl.BlockSpec(memory_space=pltpu.HBM)] * 2,
        out_specs=(
            pl.BlockSpec(memory_space=pl.ANY),
            pl.BlockSpec(memory_space=pltpu.VMEM),
        ),
        scratch_shapes=[
            field(4 * OWN), field(2 * OWN), field(4 * OWN), field(2 * OWN), field(2 * OWN), field(OWN),
            pltpu.VMEM((2 * OWN, NY, NZ), jnp.float32),
            pltpu.VMEM((4, 4, OWN, NY, NZ), jnp.float32),
            pltpu.VMEM((128, NZ), jnp.float32),
            pltpu.VMEM((64, NZ), jnp.float32),
            dma((5,)), dma((4,)), dma((4,)),
            dma((4, 3)), dma((4, 3)), dma((4, 3)), dma((4, 3)), dma((4, 2)), dma((4, 2)),
            dma((4, 3)), dma((4, 3)), dma((4,)),
            dma((63,)), dma((63,)), pltpu.SemaphoreType.REGULAR((5,)),
        ],
        compiler_params=pltpu.CompilerParams(
            collective_id=0, has_side_effects=True, vmem_limit_bytes=40 * 1024 * 1024
        ),
    )(orbitals, potential)
    return filtered, grams[0:4], grams[4:8]


def solution(mesh):
    return jax.shard_map(
        per_device,
        mesh=mesh,
        in_specs=(P("orb", "grid", None, None), P("grid", None, None)),
        out_specs=(P("orb", "grid", None, None), P("orb", None), P("orb", None)),
        check_vma=False,
    )
```
